32 devices in a mesh: dp: 16 (over z, x, core), tensor: 2 (over y).
Axes of the slice: x: 2, y: 2, z: 4, core: 2. Of those that a mesh axis runs over, the one named last changes fastest.
Arguments:
- tokens: bfloat16 [8192, 768], P('dp'), may hold values from -6 to 6
- query_weight: bfloat16 [2, 768, 768], P(None, None, 'tensor'), may hold values from -0.02734375 to 0.02734375
- key_weight: bfloat16 [2, 768, 768], P(None, None, 'tensor'), may hold values from -0.21875 to 0.21875
- value_weight: bfloat16 [2, 768, 768], P(None, None, 'tensor'), may hold values from -0.21875 to 0.21875
- output_weight: bfloat16 [2, 768, 768], P(None, 'tensor'), may hold values from -1.75 to 1.75
- prenorm_gain: bfloat16 [2, 768], replicated, may hold values from 0.5 to 1.5
- midnorm_gain: bfloat16 [2, 768], replicated, may hold values from 0.5 to 1.5
- bucket_bias_table: bfloat16 [2, 32, 12], P(None, None, 'tensor'), may hold values from -4 to 4
- router_weight: bfloat16 [2, 768, 3], replicated, may hold values from -0.15625 to 0.15625
- expert_up: bfloat16 [2, 3, 768, 3072], P(None, None, None, 'tensor'), may hold values from -0.21875 to 0.21875
- expert_down: bfloat16 [2, 3, 3072, 768], P(None, None, 'tensor'), may hold values from -0.3125 to 0.3125
- lengths: int32 [16, 4], P('dp'), may hold values from 0 to 512, as said below
- expert_ids: int32 [8192, 1], P('dp'), may hold values from 0 to 2
- cotangent: bfloat16 [8192, 768], P('dp'), may hold values from -6 to 6
Outputs:
- activations: bfloat16 [8192, 768], P('dp')
- input_grad: float32 [8192, 768], P('dp')
- query_weight_grad: float32 [2, 768, 768], P(None, 'dp', 'tensor')
- key_grad: float32 [2, 768, 768], P(None, 'dp', 'tensor')
- value_grad: float32 [2, 768, 768], P(None, 'dp', 'tensor')
- output_grad: float32 [2, 768, 768], P(None, 'tensor', 'dp')
- prenorm_grad: float32 [2, 768], P(None, 'dp')
- midnorm_grad: float32 [2, 768], P(None, 'dp')
- table_grad: float32 [2, 32, 12], P(None, None, 'tensor')
- router_grad: float32 [2, 768, 3], P(None, 'dp')
- expert_up_grad: float32 [2, 3, 768, 3072], P(None, None, 'dp', 'tensor')
- down_grad: float32 [2, 3, 3072, 768], P(None, None, 'tensor', 'dp')
The draws below stay inside these ranges and needn't reach their ends.
Inputs may be any that keep to these rules, and one draw needn't show every extreme that they name: Row r gives the lengths of the 4 sequences packed from the start of block r; a row sums to 512 or less, lengths may be 0, and some row holds one sequence of 512.
All inputs are finite; a program needn't handle non-finite values.
Results may differ from the reference program's by a relative error of at most 0.022.
Values sent between devices are 32-bit elements; how exact they have to be, the bound alone decides.
A program may use at most 320 MiB of HBM per device.

```python
import jax
import jax.numpy as jnp
from jax import lax

D = 768
HEADS = 12
HEAD_DIM = 64
FF = 3072
POSITION_BUCKETS = 32
EXPERTS = 3
LAYERS = 2
SEQS = 4
TOK_DEV = 512
CAP = 170
TOKENS = 8192
N_DP = 16


def draw_lengths(key, part):
    key = jax.random.fold_in(key, 11)
    key_total, key_cut, key_full = jax.random.split(key, 3)
    running_totals = jax.random.randint(key_total, (N_DP,), TOK_DEV // 2, TOK_DEV + 1, dtype=jnp.int32)
    cut_points = jax.random.randint(key_cut, (N_DP, SEQS - 1), 0, TOK_DEV + 1, dtype=jnp.int32)
    cut_points = jnp.sort(jnp.minimum(cut_points, running_totals[:, None]), axis=1)
    sequence_edges = jnp.concatenate([jnp.zeros((N_DP, 1), jnp.int32), cut_points, running_totals[:, None]], axis=1)
    spans = sequence_edges[:, 1:] - sequence_edges[:, :-1]
    full_row = jax.random.randint(key_full, (), 0, N_DP, dtype=jnp.int32)
    single = jnp.zeros((SEQS,), jnp.int32).at[0].set(TOK_DEV)
    row_ids = jnp.arange(N_DP, dtype=jnp.int32)
    return jnp.where((row_ids == full_row)[:, None], single[None, :], spans).astype(jnp.int32)


def with_spikes(values, own_key, source, target, parts, factor):
    def block_of(dim):
        return (jnp.arange(values.shape[dim]) // (values.shape[dim] // parts)).reshape((-1,) + (1,) * (values.ndim - 1 - dim))

    near = jax.random.permutation(own_key, parts)[block_of(target)]
    far = (block_of(target) + parts // 2) % parts
    return jnp.where((block_of(source) == near) | (block_of(source) == far), factor * values, values)


def levels(rng, dims, pieces, low, high):
    factor_of, own = 1.0, jax.random.fold_in(rng, 6)
    for axis_at, parts in pieces:
        draws = jnp.exp(jax.random.uniform(jax.random.fold_in(own, axis_at), (parts,), jnp.float32, low / len(pieces), high / len(pieces)))
        factor_of = factor_of * jnp.repeat(draws, dims[axis_at] // parts).reshape([-1 if axis == axis_at else 1 for axis in range(len(dims))])
    return factor_of


def picks_of(key, rows, amount, top, lift):
    ranking = jax.random.permutation(jax.random.fold_in(key, 1), amount)
    boost = ranking
    for power in range(3):
        boost = boost * boost // amount
    boost = boost * lift // amount
    chance = jax.random.randint(jax.random.fold_in(key, 2), (rows, amount), 0, 4096) + boost
    holders = jax.random.permutation(jax.random.fold_in(key, 3), rows)[jnp.arange(amount) % rows]
    chance = jnp.where(jnp.arange(rows)[:, None] == holders[None, :], 1 << 14, chance)
    merit = chance * amount + jnp.arange(amount)
    return lax.top_k(merit.astype(jnp.int32), top)[1].astype(jnp.int32)


def normal_values(stream_key, dims, spread, most, shards=(), kind=jnp.bfloat16):
    drawn = spread * jax.random.normal(stream_key, dims, jnp.float32)
    if shards:
        drawn = drawn * levels(stream_key, dims, shards, -0.22, 0.18)
    return jnp.clip(drawn, -most, most).astype(kind)


def gaussian_with(own_key, extent, width, reach, cuts, heavy, kind=jnp.bfloat16):
    result = width * jax.random.normal(own_key, extent, jnp.float32)
    if cuts:
        result = result * levels(own_key, extent, cuts, -0.22, 0.18)
    return jnp.clip(with_spikes(result, jax.random.fold_in(own_key, 3), *heavy), -reach, reach).astype(kind)


def setup_inputs(seed: int = 0) -> dict:
    streams_of = jax.random.split(jax.random.key(seed), 15)
    tokens = normal_values(streams_of[0], (TOKENS, D), 1.0, 6.0, ((0, 16),))
    query_weight = normal_values(streams_of[1], (LAYERS, D, HEADS * HEAD_DIM), (D * HEAD_DIM) ** -0.5, 0.02734375, ((2, 2),))
    key_weight = normal_values(streams_of[2], (LAYERS, D, HEADS * HEAD_DIM), D ** -0.5, 0.21875, ((2, 2),))
    value_weight = normal_values(streams_of[3], (LAYERS, D, HEADS * HEAD_DIM), D ** -0.5, 0.21875, ((2, 2),))
    output_weight = normal_values(streams_of[4], (LAYERS, HEADS * HEAD_DIM, D), (HEADS * HEAD_DIM // 64) ** -0.5, 1.75, ((1, 2),))
    prenorm_gain = jnp.clip(1.0 + 0.1 * jax.random.normal(streams_of[5], (LAYERS, D), jnp.float32), 0.5, 1.5).astype(jnp.bfloat16)
    midnorm_gain = jnp.clip(1.0 + 0.1 * jax.random.normal(streams_of[6], (LAYERS, D), jnp.float32), 0.5, 1.5).astype(jnp.bfloat16)
    bucket_bias_table = normal_values(streams_of[7], (LAYERS, POSITION_BUCKETS, HEADS), 1.0, 4.0, ((2, 2),))
    router_weight = normal_values(streams_of[8], (LAYERS, D, EXPERTS), (2 * D) ** -0.5, 0.15625)
    expert_up = normal_values(streams_of[9], (LAYERS, EXPERTS, D, FF), D ** -0.5, 0.21875, ((3, 2),))
    expert_down = normal_values(streams_of[10], (LAYERS, EXPERTS, FF, D), (FF // 8) ** -0.5, 0.3125, ((2, 2),))
    lengths = draw_lengths(jax.random.fold_in(streams_of[14], 71), 0)
    expert_ids = picks_of(streams_of[12], TOKENS, EXPERTS, 1, 2730)
    cotangent = gaussian_with(streams_of[13], (TOKENS, D), 1.0, 6.0, ((0, 16),), (0, 1, 16, 2.0))
    return {"tokens": tokens, "query_weight": query_weight, "key_weight": key_weight, "value_weight": value_weight, "output_weight": output_weight, "prenorm_gain": prenorm_gain, "midnorm_gain": midnorm_gain, "bucket_bias_table": bucket_bias_table, "router_weight": router_weight, "expert_up": expert_up, "expert_down": expert_down, "lengths": lengths, "expert_ids": expert_ids, "cotangent": cotangent}


@jax.custom_vjp
def low(v):
    return lax.optimization_barrier(v.astype(jnp.bfloat16)).astype(jnp.float32)

@jax.custom_vjp
def low_back(v):
    return v

def low_keep(v):
    return (low(v), None)

def low_pass(kept, grad):
    return (grad,)

def back_keep(v):
    return (v, None)

def back_low(kept, grad):
    return (low(grad),)
low.defvjp(low_keep, low_pass)
low_back.defvjp(back_keep, back_low)
LIMITS = (12, 16, 23, 32, 46, 64, 91)
EPSILON = 1e-06
PRECISE = lax.Precision.HIGHEST

def bucket_ids(query_pos, key_pos):
    relative = key_pos[None, :] - query_pos[:, None]
    distance = jnp.abs(relative)
    beyond = 8 + sum(((distance >= limit_at).astype(jnp.int32) for limit_at in LIMITS))
    return jnp.where(distance < 8, distance, beyond) + 16 * (relative > 0).astype(jnp.int32)

def rms_norm(stream, scale_gain):
    return stream * lax.rsqrt(lax.optimization_barrier(jnp.mean(stream * stream, axis=-1, keepdims=True)) + EPSILON) * scale_gain

def segments(length_row, row_count):
    ends_at = jnp.cumsum(length_row.astype(jnp.int32), dtype=jnp.int32)
    position = jnp.arange(row_count, dtype=jnp.int32)
    segment = lax.optimization_barrier(jnp.sum((position[:, None] >= ends_at[None, :]).astype(jnp.int32), axis=1, dtype=jnp.int32))
    alive_rows = position < ends_at[-1]
    return (jnp.where(alive_rows, segment, -1), alive_rows)

def slot_of(expert_pick, alive_rows):
    picked_expert = ((expert_pick[:, None] == jnp.arange(EXPERTS, dtype=jnp.int32)[None, :]) & alive_rows[:, None]).astype(jnp.int32)
    prior_value = jnp.cumsum(picked_expert, axis=0, dtype=jnp.int32) - picked_expert
    position = lax.optimization_barrier(jnp.sum(prior_value * picked_expert, axis=1, dtype=jnp.int32))
    return jnp.where(alive_rows & (position < CAP), position, CAP)

def round_both(values):
    return low(low_back(values))

def attend(query_split, key_split, value_split, table_layer, segment):
    row_count = query_split.shape[0]
    position = jnp.arange(row_count, dtype=jnp.int32)
    bucket_map = bucket_ids(position, position)
    pos_bias = jnp.transpose(table_layer, (1, 0))[:, bucket_map]
    scores = low_back(jnp.einsum('qhd,khd->hqk', query_split, key_split, precision=PRECISE) + pos_bias)
    same_sequence = segment[:, None] == segment[None, :]
    scores = jnp.where(same_sequence[None], scores, -1000000000.0)
    attn_probs = low(jax.nn.softmax(scores, axis=-1))
    return jnp.einsum('hqk,khd->qhd', attn_probs, value_split, precision=PRECISE).reshape(row_count, -1)

def layers(stream, params, segment, expert_pick, expert_slot_index):
    query_weight, key_weight, value_weight, output_weight, prenorm_gain, midnorm_gain, bucket_bias_table, router_weight, expert_up, expert_down = params
    row_count = stream.shape[0]
    picked_expert = (expert_pick[:, None] == jnp.arange(EXPERTS, dtype=jnp.int32)[None, :]).astype(jnp.float32)
    for layer_index in range(LAYERS):
        normed = low(rms_norm(stream, prenorm_gain[layer_index]))
        query_split = round_both(jnp.dot(normed, query_weight[layer_index], precision=PRECISE)).reshape(row_count, HEADS, HEAD_DIM)
        key_split = round_both(jnp.dot(normed, key_weight[layer_index], precision=PRECISE)).reshape(row_count, HEADS, HEAD_DIM)
        value_split = round_both(jnp.dot(normed, value_weight[layer_index], precision=PRECISE)).reshape(row_count, HEADS, HEAD_DIM)
        mixed_heads = round_both(attend(query_split, key_split, value_split, bucket_bias_table[layer_index], segment))
        stream = stream + low_back(jnp.dot(mixed_heads, output_weight[layer_index], precision=PRECISE))
        second = low(rms_norm(stream, midnorm_gain[layer_index]))
        router_probs = jax.nn.softmax(jnp.dot(second, router_weight[layer_index], precision=PRECISE), axis=-1)
        gate_prob = lax.optimization_barrier(jnp.sum(router_probs * picked_expert, axis=-1, keepdims=True))
        dispatched = jnp.zeros((EXPERTS, CAP + 1, D), jnp.float32).at[expert_pick, expert_slot_index].add(second)[:, :CAP]
        hidden = low_back(jnp.einsum('ecd,edf->ecf', dispatched, expert_up[layer_index], precision=PRECISE))
        active = low(jax.nn.gelu(hidden, approximate=True))
        expert_rows = jnp.einsum('ecf,efd->ecd', active, expert_down[layer_index], precision=PRECISE)
        expert_rows = jnp.concatenate([expert_rows, jnp.zeros((EXPERTS, 1, D), jnp.float32)], axis=1)
        stream = stream + gate_prob * low_back(expert_rows[expert_pick, expert_slot_index])
    return stream

def reference(tokens, query_weight, key_weight, value_weight, output_weight, prenorm_gain, midnorm_gain, bucket_bias_table, router_weight, expert_up, expert_down, lengths, expert_ids, cotangent):
    params = tuple((weight_arr.astype(jnp.float32) for weight_arr in (query_weight, key_weight, value_weight, output_weight, prenorm_gain, midnorm_gain, bucket_bias_table, router_weight, expert_up, expert_down)))
    stream_rows = tokens.astype(jnp.float32).reshape(N_DP, TOK_DEV, D)
    upstream_rows = cotangent.astype(jnp.float32).reshape(N_DP, TOK_DEV, D)
    pick_rows = expert_ids.reshape(N_DP, TOK_DEV)

    def row_step(running_totals, inputs):
        stream, upstream, length_row, expert_pick = inputs
        segment, alive_rows = segments(length_row, TOK_DEV)
        expert_slot_index = slot_of(expert_pick, alive_rows)

        def forward(stream_in, param_set):
            return layers(stream_in, param_set, segment, expert_pick, expert_slot_index)
        result_row, pullback = jax.vjp(forward, stream, params)
        stream_grad, param_grads = pullback(upstream * alive_rows[:, None].astype(jnp.float32))
        running_totals = jax.tree.map(jnp.add, running_totals, param_grads)
        return (running_totals, (result_row.astype(jnp.bfloat16), stream_grad))
    initial = tuple((jnp.zeros_like(param_arr) for param_arr in params))
    running_totals, (result_rows, grad_rows) = lax.scan(row_step, initial, (stream_rows, upstream_rows, lengths, pick_rows))
    query_weight_grad, key_grad, value_grad, output_grad, prenorm_grad, midnorm_grad, table_grad, router_grad, expert_up_grad, down_grad = running_totals
    return (result_rows.reshape(TOKENS, D), grad_rows.reshape(TOKENS, D), query_weight_grad, key_grad, value_grad, output_grad, prenorm_grad, midnorm_grad, table_grad, router_grad, expert_up_grad, down_grad)
```

```python
import jax
import jax.numpy as jnp
from jax import lax
from jax.sharding import PartitionSpec as P

POSITION_BUCKETS = 32
EXPERTS = 3
LAYERS = 2
CAP = 170


LIMITS = (12, 16, 23, 32, 46, 64, 91)
EPSILON = 1e-06
CAP_PADDED = 176
PRECISE = lax.Precision.HIGHEST


def bucket_ids(query_pos, key_pos):
    relative = key_pos[None, :] - query_pos[:, None]
    distance = jnp.abs(relative)
    beyond = 8 + sum(((distance >= limit_at).astype(jnp.int32) for limit_at in LIMITS))
    return jnp.where(distance < 8, distance, beyond) + 16 * (relative > 0).astype(jnp.int32)


def rms_norm(stream, scale_gain):
    return (
        stream * lax.rsqrt(jnp.mean(stream * stream, axis=-1, keepdims=True) + EPSILON) * scale_gain
    )


def gelu_tanh(values):
    return jax.nn.gelu(values, approximate=True)


def segments(length_row, row_count):
    ends_at = jnp.cumsum(length_row, dtype=jnp.int32)
    position = jnp.arange(row_count, dtype=jnp.int32)
    segment = jnp.sum(
        (position[:, None] >= ends_at[None, :]).astype(jnp.int32), axis=1, dtype=jnp.int32
    )
    alive_rows = position < ends_at[-1]
    return (jnp.where(alive_rows, segment, -1), alive_rows)


def slot_of(expert_pick, alive_rows):
    picked_expert = (
        (expert_pick[:, None] == jnp.arange(EXPERTS, dtype=jnp.int32)[None, :])
        & alive_rows[:, None]
    ).astype(jnp.int32)
    prior_value = jnp.cumsum(picked_expert, axis=0, dtype=jnp.int32) - picked_expert
    position = jnp.sum(prior_value * picked_expert, axis=1, dtype=jnp.int32)
    return jnp.where(alive_rows & (position < CAP), position, CAP)


def exchange_sum(partial_value):
    tensor_size = lax.axis_size("tensor")
    total = partial_value
    for shift in range(1, tensor_size):
        pairs = [(at, (at + shift) % tensor_size) for at in range(tensor_size)]
        total = total + lax.ppermute(partial_value, "tensor", pairs)
    return total


def flip_pairs(size, bit):
    return [(at, at ^ (1 << bit)) for at in range(size)]


def relative_order(model_width):
    size = lax.axis_size("dp")
    bit_count = size.bit_length() - 1
    width = model_width // size
    column = jnp.arange(model_width, dtype=jnp.int32)
    place = column // width
    mask = sum(((place >> (bit_count - 1 - bit)) & 1) << bit for bit in range(bit_count))
    source = (mask ^ lax.axis_index("dp")) * width + column % width
    return (column[:, None] == source[None, :]).astype(jnp.bfloat16)


def scatter_sum(term_of, model_width):
    size = lax.axis_size("dp")
    bit_count = size.bit_length() - 1
    half = model_width // 2
    received = lax.ppermute(term_of(half, model_width), "dp", flip_pairs(size, 0))
    if bit_count == 1:
        return term_of(0, half) + received
    quarter = half // 2
    sent = term_of(quarter, half) + received[..., quarter:, :]
    kept = term_of(0, quarter) + received[..., :quarter, :]
    for bit in range(1, bit_count):
        received = lax.ppermute(sent, "dp", flip_pairs(size, bit))
        if bit == bit_count - 1:
            return kept + received
        middle_row = kept.shape[-2] // 2
        sent = kept[..., middle_row:, :] + received[..., middle_row:, :]
        kept = kept[..., :middle_row, :] + received[..., :middle_row, :]


def doubling_sum(values):
    size = lax.axis_size("dp")
    for bit in range(size.bit_length() - 1):
        values = values + lax.ppermute(values, "dp", flip_pairs(size, bit))
    return values


def rows_of_slots(slot_indicator, slot_rows):
    upper = lax.reduce_precision(slot_rows, 8, 7)
    lower = slot_rows - upper
    return sum(
        jnp.einsum(
            "kt,kd->td",
            slot_indicator,
            part.astype(jnp.bfloat16),
            preferred_element_type=jnp.float32,
        )
        for part in (upper, lower)
    )


def attention_scores(query_rows, key_rows, bucket_bias_table, segment, bucket_indicator):
    row_count = query_rows.shape[0]
    heads_here = bucket_bias_table.shape[1]
    pos_bias = jnp.einsum(
        "cgp,cf->fgp", bucket_indicator, bucket_bias_table, preferred_element_type=jnp.float32
    )
    query_split = query_rows.reshape(row_count, heads_here, -1)
    key_split = key_rows.reshape(row_count, heads_here, -1)
    scores = (
        jnp.einsum("qhd,khd->hqk", query_split, key_split, preferred_element_type=jnp.float32)
        + pos_bias
    )
    same_sequence = segment[:, None] == segment[None, :]
    return jnp.where(same_sequence[None], scores, -1000000000.0)


def forward_layer(
    stream, weight_set, segment, expert_pick, slot_indicator, bucket_indicator
):
    (
        query_weight,
        key_weight,
        value_weight,
        output_weight,
        prenorm_gain,
        midnorm_gain,
        bucket_bias_table,
        router_weight,
        expert_up,
        expert_down,
    ) = weight_set
    row_count, model_width = stream.shape
    heads_here = bucket_bias_table.shape[1]
    normed = rms_norm(stream, prenorm_gain.astype(jnp.float32)).astype(jnp.bfloat16)
    query_rows = jnp.dot(normed, query_weight, preferred_element_type=jnp.float32).astype(
        jnp.bfloat16
    )
    key_rows = jnp.dot(normed, key_weight, preferred_element_type=jnp.float32).astype(jnp.bfloat16)
    value_rows = jnp.dot(normed, value_weight, preferred_element_type=jnp.float32).astype(
        jnp.bfloat16
    )
    scores = attention_scores(query_rows, key_rows, bucket_bias_table, segment, bucket_indicator)
    row_peak = jnp.max(scores, axis=-1, keepdims=True)
    exponentiated = jnp.exp(scores - row_peak)
    row_total = jnp.sum(exponentiated, axis=-1, keepdims=True)
    attn_probs = (exponentiated / row_total).astype(jnp.bfloat16)
    value_split = value_rows.reshape(row_count, heads_here, -1)
    mixed_heads = (
        jnp.einsum("hqk,khd->qhd", attn_probs, value_split, preferred_element_type=jnp.float32)
        .reshape(row_count, -1)
        .astype(jnp.bfloat16)
    )
    log_total = row_peak + jnp.log(row_total)
    partial_value = jnp.dot(mixed_heads, output_weight, preferred_element_type=jnp.float32)
    middle = stream + exchange_sum(partial_value)
    second = rms_norm(middle, midnorm_gain.astype(jnp.float32)).astype(jnp.bfloat16)
    logits = jnp.dot(second, router_weight, preferred_element_type=jnp.float32)
    router_probs = jax.nn.softmax(logits, axis=-1)
    picked_expert = (expert_pick[:, None] == jnp.arange(EXPERTS, dtype=jnp.int32)[None, :]).astype(
        jnp.float32
    )
    gate_prob = jnp.sum(router_probs * picked_expert, axis=-1, keepdims=True)
    dispatched = jnp.dot(slot_indicator, second).reshape(EXPERTS, CAP_PADDED, model_width)
    hidden = jnp.einsum("ecd,edf->ecf", dispatched, expert_up, preferred_element_type=jnp.float32)
    active = gelu_tanh(hidden).astype(jnp.bfloat16)
    expert_rows = jnp.einsum(
        "ecf,efd->ecd", active, expert_down, preferred_element_type=jnp.float32
    )
    combined = exchange_sum(
        rows_of_slots(slot_indicator, expert_rows.reshape(-1, model_width))
    )
    saved_state = (
        stream,
        normed,
        query_rows,
        key_rows,
        value_rows,
        mixed_heads,
        log_total,
        middle,
        second,
        router_probs,
        gate_prob,
        dispatched,
        hidden,
        active,
        combined,
    )
    return (saved_state, middle + gate_prob * combined)


def layer_backward_pass(
    upstream,
    saved_state,
    weight_set,
    segment,
    expert_pick,
    slot_indicator,
    bucket_indicator,
    order,
):
    (
        query_weight,
        key_weight,
        value_weight,
        output_weight,
        prenorm_gain,
        midnorm_gain,
        bucket_bias_table,
        router_weight,
        expert_up,
        expert_down,
    ) = weight_set
    (
        stream,
        normed,
        query_rows,
        key_rows,
        value_rows,
        mixed_heads,
        log_total,
        middle,
        second,
        router_probs,
        gate_prob,
        dispatched,
        hidden,
        active,
        combined,
    ) = saved_state
    row_count, model_width = stream.shape
    heads_here = bucket_bias_table.shape[1]
    picked_expert = (expert_pick[:, None] == jnp.arange(EXPERTS, dtype=jnp.int32)[None, :]).astype(
        jnp.float32
    )
    combined_grad = (gate_prob * upstream).astype(jnp.bfloat16)
    gate_grad = jnp.sum(upstream * combined, axis=-1, keepdims=True)
    logit_grad = gate_grad * gate_prob * (picked_expert - router_probs)
    router_term = jnp.dot(second.astype(jnp.float32).T, logit_grad, precision=PRECISE)
    second_grad = jnp.dot(logit_grad, router_weight.astype(jnp.float32).T, precision=PRECISE)
    slot_grad = jnp.dot(slot_indicator, combined_grad).reshape(EXPERTS, CAP_PADDED, model_width)
    active_grad = jnp.einsum(
        "ecd,efd->ecf", slot_grad, expert_down, preferred_element_type=jnp.float32
    )
    hidden_grad = jax.vjp(gelu_tanh, hidden)[1](active_grad)[0].astype(jnp.bfloat16)
    dispatch_grad = jnp.einsum(
        "ecf,edf->ecd", hidden_grad, expert_up, preferred_element_type=jnp.float32
    )
    second_grad = second_grad + exchange_sum(
        rows_of_slots(slot_indicator, dispatch_grad.reshape(-1, model_width))
    )
    slot_grad_ordered = jnp.dot(slot_grad, order)
    dispatched_ordered = jnp.dot(dispatched, order)

    def expert_term(ordered, hidden_rows):
        def term_of(low, high):
            return jnp.einsum(
                "cd,cf->df", ordered[:, low:high], hidden_rows, preferred_element_type=jnp.float32
            )

        return scatter_sum(term_of, model_width)

    down_term = jnp.stack(
        [expert_term(slot_grad_ordered[at], active[at]).T for at in range(EXPERTS)]
    )
    up_term = jnp.stack(
        [expert_term(dispatched_ordered[at], hidden_grad[at]) for at in range(EXPERTS)]
    )
    middle_grad, midnorm_term = jax.vjp(rms_norm, middle, midnorm_gain.astype(jnp.float32))[1](
        second_grad
    )
    middle_grad = upstream + middle_grad
    attn_grad = middle_grad.astype(jnp.bfloat16)
    output_term = expert_term(jnp.dot(attn_grad, order), mixed_heads).T
    mixed_grad = jnp.einsum(
        "td,fd->tf", attn_grad, output_weight, preferred_element_type=jnp.float32
    ).astype(jnp.bfloat16)
    scores = attention_scores(query_rows, key_rows, bucket_bias_table, segment, bucket_indicator)
    attn_probs = jnp.exp(scores - log_total)
    probs_low = attn_probs.astype(jnp.bfloat16)
    query_split = query_rows.reshape(row_count, heads_here, -1)
    key_split = key_rows.reshape(row_count, heads_here, -1)
    value_split = value_rows.reshape(row_count, heads_here, -1)
    mixed_split = mixed_grad.reshape(row_count, heads_here, -1)
    probs_grad = jnp.einsum(
        "qhd,khd->hqk", mixed_split, value_split, preferred_element_type=jnp.float32
    )
    center = jnp.sum(attn_probs * probs_grad, axis=-1, keepdims=True)
    score_gradient = (attn_probs * (probs_grad - center)).astype(jnp.bfloat16)
    value_back = jnp.einsum(
        "hqk,qhd->khd", probs_low, mixed_split, preferred_element_type=jnp.float32
    )
    key_back = jnp.einsum(
        "hqk,qhd->khd", score_gradient, query_split, preferred_element_type=jnp.float32
    )
    query_back = jnp.einsum(
        "hqk,khd->qhd", score_gradient, key_split, preferred_element_type=jnp.float32
    )
    table_term = jnp.einsum(
        "esm,psm->pe", score_gradient, bucket_indicator, preferred_element_type=jnp.float32
    )
    query_back = query_back.reshape(row_count, -1).astype(jnp.bfloat16)
    key_back = key_back.reshape(row_count, -1).astype(jnp.bfloat16)
    value_back = value_back.reshape(row_count, -1).astype(jnp.bfloat16)
    projection_term = expert_term(
        jnp.dot(normed, order), jnp.concatenate([query_back, key_back, value_back], axis=1)
    )
    query_term, key_term, value_term = jnp.split(projection_term, 3, axis=1)
    normed_part = (
        jnp.einsum("tf,df->td", query_back, query_weight, preferred_element_type=jnp.float32)
        + jnp.einsum("tf,df->td", key_back, key_weight, preferred_element_type=jnp.float32)
        + jnp.einsum("tf,df->td", value_back, value_weight, preferred_element_type=jnp.float32)
    )
    normed_grad = exchange_sum(normed_part)
    stream_grad, prenorm_term = jax.vjp(rms_norm, stream, prenorm_gain.astype(jnp.float32))[1](
        normed_grad
    )
    term_set = (
        query_term,
        key_term,
        value_term,
        output_term,
        prenorm_term,
        midnorm_term,
        table_term,
        router_term,
        up_term,
        down_term,
    )
    return (middle_grad + stream_grad, term_set)


def on_device(
    tokens,
    query_weight,
    key_weight,
    value_weight,
    output_weight,
    prenorm_gain,
    midnorm_gain,
    bucket_bias_table,
    router_weight,
    expert_up,
    expert_down,
    lengths,
    expert_ids,
    cotangent,
):
    row_count = tokens.shape[0]
    segment, alive_rows = segments(lengths[0], row_count)
    expert_pick = expert_ids[:, 0]
    expert_slot_index = slot_of(expert_pick, alive_rows)
    flat_slot = jnp.where(
        expert_slot_index < CAP, expert_pick * CAP_PADDED + expert_slot_index, -1
    )
    slot_indicator = (
        jnp.arange(EXPERTS * CAP_PADDED, dtype=jnp.int32)[:, None] == flat_slot[None, :]
    ).astype(jnp.bfloat16)
    order = relative_order(tokens.shape[1])
    position = jnp.arange(row_count, dtype=jnp.int32)
    bucket_map = bucket_ids(position, position)
    bucket_indicator = (
        bucket_map[None] == jnp.arange(POSITION_BUCKETS, dtype=jnp.int32)[:, None, None]
    ).astype(jnp.bfloat16)
    weight_all = (
        query_weight,
        key_weight,
        value_weight,
        output_weight,
        prenorm_gain,
        midnorm_gain,
        bucket_bias_table,
        router_weight,
        expert_up,
        expert_down,
    )
    stream = tokens.astype(jnp.float32)
    saved_list = []
    for layer_index in range(LAYERS):
        weight_set = tuple((weight_arr[layer_index] for weight_arr in weight_all))
        saved_state, stream = forward_layer(
            stream, weight_set, segment, expert_pick, slot_indicator, bucket_indicator
        )
        saved_list.append(saved_state)
    upstream = cotangent.astype(jnp.float32) * alive_rows[:, None].astype(jnp.float32)
    layer_terms = [None] * LAYERS
    for layer_index in reversed(range(LAYERS)):
        weight_set = tuple((weight_arr[layer_index] for weight_arr in weight_all))
        upstream, term_set = layer_backward_pass(
            upstream,
            saved_list[layer_index],
            weight_set,
            segment,
            expert_pick,
            slot_indicator,
            bucket_indicator,
            order,
        )
        layer_terms[layer_index] = term_set
    (
        query_weight_grad,
        key_grad,
        value_grad,
        output_grad,
        prenorm_grad,
        midnorm_grad,
        table_grad,
        router_grad,
        expert_up_grad,
        down_grad,
    ) = tuple(
        (
            jnp.stack([layer_terms[layer_index][member] for layer_index in range(LAYERS)])
            for member in range(10)
        )
    )
    model_width = tokens.shape[1]
    heads_here = bucket_bias_table.shape[2]
    small = jnp.concatenate(
        [
            prenorm_grad,
            midnorm_grad,
            router_grad.transpose(2, 0, 1).reshape(EXPERTS * LAYERS, model_width),
            jnp.pad(
                table_grad.reshape(LAYERS, -1),
                ((0, 0), (0, model_width - POSITION_BUCKETS * heads_here)),
            ),
        ]
    )
    small = doubling_sum(small)
    width = model_width // lax.axis_size("dp")
    own = lax.dynamic_slice_in_dim(
        small[: (2 + EXPERTS) * LAYERS], lax.axis_index("dp") * width, width, axis=1
    )
    prenorm_grad = own[:LAYERS]
    midnorm_grad = own[LAYERS : 2 * LAYERS]
    router_grad = own[2 * LAYERS :].reshape(EXPERTS, LAYERS, width).transpose(1, 2, 0)
    table_grad = small[(2 + EXPERTS) * LAYERS :, : POSITION_BUCKETS * heads_here].reshape(
        LAYERS, POSITION_BUCKETS, heads_here
    )
    return (
        stream.astype(jnp.bfloat16),
        upstream,
        query_weight_grad,
        key_grad,
        value_grad,
        output_grad,
        prenorm_grad,
        midnorm_grad,
        table_grad,
        router_grad,
        expert_up_grad,
        down_grad,
    )


def solution(mesh):
    return jax.shard_map(
        on_device,
        mesh=mesh,
        in_specs=(
            P("dp", None),
            P(None, None, "tensor"),
            P(None, None, "tensor"),
            P(None, None, "tensor"),
            P(None, "tensor", None),
            P(),
            P(),
            P(None, None, "tensor"),
            P(),
            P(None, None, None, "tensor"),
            P(None, None, "tensor", None),
            P("dp", None),
            P("dp", None),
            P("dp", None),
        ),
        out_specs=(
            P("dp", None),
            P("dp", None),
            P(None, "dp", "tensor"),
            P(None, "dp", "tensor"),
            P(None, "dp", "tensor"),
            P(None, "tensor", "dp"),
            P(None, "dp"),
            P(None, "dp"),
            P(None, None, "tensor"),
            P(None, "dp", None),
            P(None, None, "dp", "tensor"),
            P(None, None, "tensor", "dp"),
        ),
        check_vma=False,
    )
```

```python
import jax
import jax.numpy as jnp
from jax import lax
from jax.sharding import PartitionSpec as P

POSITION_BUCKETS = 32
EXPERTS = 3
LAYERS = 2
CAP = 170


LIMITS = (12, 16, 23, 32, 46, 64, 91)
EPSILON = 1e-06
CAP_PADDED = 176
PRECISE = lax.Precision.HIGHEST


def bucket_ids(query_pos, key_pos):
    relative = key_pos[None, :] - query_pos[:, None]
    distance = jnp.abs(relative)
    beyond = 8 + sum(((distance >= limit_at).astype(jnp.int32) for limit_at in LIMITS))
    return jnp.where(distance < 8, distance, beyond) + 16 * (relative > 0).astype(jnp.int32)


def rms_norm(stream, scale_gain):
    return (
        stream * lax.rsqrt(jnp.mean(stream * stream, axis=-1, keepdims=True) + EPSILON) * scale_gain
    )


def gelu_tanh(values):
    return jax.nn.gelu(values, approximate=True)


def segments(length_row, row_count):
    ends_at = jnp.cumsum(length_row, dtype=jnp.int32)
    position = jnp.arange(row_count, dtype=jnp.int32)
    segment = jnp.sum(
        (position[:, None] >= ends_at[None, :]).astype(jnp.int32), axis=1, dtype=jnp.int32
    )
    alive_rows = position < ends_at[-1]
    return (jnp.where(alive_rows, segment, -1), alive_rows)


def slot_of(expert_pick, alive_rows):
    picked_expert = (
        (expert_pick[:, None] == jnp.arange(EXPERTS, dtype=jnp.int32)[None, :])
        & alive_rows[:, None]
    ).astype(jnp.int32)
    prior_value = jnp.cumsum(picked_expert, axis=0, dtype=jnp.int32) - picked_expert
    position = jnp.sum(prior_value * picked_expert, axis=1, dtype=jnp.int32)
    return jnp.where(alive_rows & (position < CAP), position, CAP)


def exchange_sum(partial_value):
    tensor_size = lax.axis_size("tensor")
    total = partial_value
    for shift in range(1, tensor_size):
        pairs = [(at, (at + shift) % tensor_size) for at in range(tensor_size)]
        total = total + lax.ppermute(partial_value, "tensor", pairs)
    return total


def flip_pairs(size, bit):
    return [(at, at ^ (1 << bit)) for at in range(size)]


def relative_order(model_width):
    size = lax.axis_size("dp")
    bit_count = size.bit_length() - 1
    width = model_width // size
    column = jnp.arange(model_width, dtype=jnp.int32)
    place = column // width
    mask = sum(((place >> (bit_count - 1 - bit)) & 1) << bit for bit in range(bit_count))
    source = (mask ^ lax.axis_index("dp")) * width + column % width
    return (column[:, None] == source[None, :]).astype(jnp.bfloat16)


class ScatterSum:
    def __init__(self, term_of, model_width):
        self.size = lax.axis_size("dp")
        self.term_of = term_of
        self.half = model_width // 2
        self.sent = term_of(self.half, model_width)
        self.kept = None
        self.bit = 0

    def step(self, after=None):
        if self.bit == self.size.bit_length() - 1:
            return
        sent = self.sent
        if after is not None:
            sent, _ = lax.optimization_barrier((sent, after))
        received = lax.ppermute(sent, "dp", flip_pairs(self.size, self.bit))
        self.bit += 1
        if self.bit == 1:
            low_half = self.half // 2
            self.sent = self.term_of(low_half, self.half) + received[low_half:]
            self.kept = self.term_of(0, low_half) + received[:low_half]
            return
        total = (self.kept, received)
        if self.bit == self.size.bit_length() - 1:
            self.kept = total[0] + total[1]
            return
        low_half = received.shape[0] // 2
        self.sent = total[0][low_half:] + total[1][low_half:]
        self.kept = total[0][:low_half] + total[1][:low_half]


def step_all(group, after=None):
    for one in group:
        one.step(after)


def doubling_sum(values):
    size = lax.axis_size("dp")
    for bit in range(size.bit_length() - 1):
        values = values + lax.ppermute(values, "dp", flip_pairs(size, bit))
    return values


def rows_of_slots(slot_indicator, slot_rows):
    upper = lax.reduce_precision(slot_rows, 8, 7)
    lower = slot_rows - upper
    return sum(
        jnp.einsum(
            "kt,kd->td",
            slot_indicator,
            part.astype(jnp.bfloat16),
            preferred_element_type=jnp.float32,
        )
        for part in (upper, lower)
    )


def attention_scores(query_rows, key_rows, bucket_bias_table, segment, bucket_indicator):
    row_count = query_rows.shape[0]
    heads_here = bucket_bias_table.shape[1]
    pos_bias = jnp.einsum(
        "cgp,cf->fgp", bucket_indicator, bucket_bias_table, preferred_element_type=jnp.float32
    )
    query_split = query_rows.reshape(row_count, heads_here, -1)
    key_split = key_rows.reshape(row_count, heads_here, -1)
    scores = (
        jnp.einsum("qhd,khd->hqk", query_split, key_split, preferred_element_type=jnp.float32)
        + pos_bias
    )
    same_sequence = segment[:, None] == segment[None, :]
    return jnp.where(same_sequence[None], scores, -1000000000.0)


def forward_layer(
    stream, weight_set, segment, expert_pick, slot_indicator, bucket_indicator
):
    (
        query_weight,
        key_weight,
        value_weight,
        output_weight,
        prenorm_gain,
        midnorm_gain,
        bucket_bias_table,
        router_weight,
        expert_up,
        expert_down,
    ) = weight_set
    row_count, model_width = stream.shape
    heads_here = bucket_bias_table.shape[1]
    normed = rms_norm(stream, prenorm_gain.astype(jnp.float32)).astype(jnp.bfloat16)
    query_rows = jnp.dot(normed, query_weight, preferred_element_type=jnp.float32).astype(
        jnp.bfloat16
    )
    key_rows = jnp.dot(normed, key_weight, preferred_element_type=jnp.float32).astype(jnp.bfloat16)
    value_rows = jnp.dot(normed, value_weight, preferred_element_type=jnp.float32).astype(
        jnp.bfloat16
    )
    scores = attention_scores(query_rows, key_rows, bucket_bias_table, segment, bucket_indicator)
    row_peak = jnp.max(scores, axis=-1, keepdims=True)
    exponentiated = jnp.exp(scores - row_peak)
    row_total = jnp.sum(exponentiated, axis=-1, keepdims=True)
    attn_probs = (exponentiated / row_total).astype(jnp.bfloat16)
    value_split = value_rows.reshape(row_count, heads_here, -1)
    mixed_heads = (
        jnp.einsum("hqk,khd->qhd", attn_probs, value_split, preferred_element_type=jnp.float32)
        .reshape(row_count, -1)
        .astype(jnp.bfloat16)
    )
    log_total = row_peak + jnp.log(row_total)
    partial_value = jnp.dot(mixed_heads, output_weight, preferred_element_type=jnp.float32)
    middle = stream + exchange_sum(partial_value)
    second = rms_norm(middle, midnorm_gain.astype(jnp.float32)).astype(jnp.bfloat16)
    logits = jnp.dot(second, router_weight, preferred_element_type=jnp.float32)
    router_probs = jax.nn.softmax(logits, axis=-1)
    picked_expert = (expert_pick[:, None] == jnp.arange(EXPERTS, dtype=jnp.int32)[None, :]).astype(
        jnp.float32
    )
    gate_prob = jnp.sum(router_probs * picked_expert, axis=-1, keepdims=True)
    dispatched = jnp.dot(slot_indicator, second).reshape(EXPERTS, CAP_PADDED, model_width)
    hidden = jnp.einsum("ecd,edf->ecf", dispatched, expert_up, preferred_element_type=jnp.float32)
    active = gelu_tanh(hidden).astype(jnp.bfloat16)
    expert_rows = jnp.einsum(
        "ecf,efd->ecd", active, expert_down, preferred_element_type=jnp.float32
    )
    combined = exchange_sum(
        rows_of_slots(slot_indicator, expert_rows.reshape(-1, model_width))
    )
    saved_state = (
        stream,
        normed,
        query_rows,
        key_rows,
        value_rows,
        mixed_heads,
        log_total,
        middle,
        second,
        router_probs,
        gate_prob,
        dispatched,
        hidden,
        active,
        combined,
    )
    return (saved_state, middle + gate_prob * combined)


def layer_backward_pass(
    upstream,
    saved_state,
    weight_set,
    segment,
    expert_pick,
    slot_indicator,
    bucket_indicator,
    order,
    earlier,
):
    (
        query_weight,
        key_weight,
        value_weight,
        output_weight,
        prenorm_gain,
        midnorm_gain,
        bucket_bias_table,
        router_weight,
        expert_up,
        expert_down,
    ) = weight_set
    (
        stream,
        normed,
        query_rows,
        key_rows,
        value_rows,
        mixed_heads,
        log_total,
        middle,
        second,
        router_probs,
        gate_prob,
        dispatched,
        hidden,
        active,
        combined,
    ) = saved_state
    row_count, model_width = stream.shape
    heads_here = bucket_bias_table.shape[1]
    picked_expert = (expert_pick[:, None] == jnp.arange(EXPERTS, dtype=jnp.int32)[None, :]).astype(
        jnp.float32
    )
    combined_grad = (gate_prob * upstream).astype(jnp.bfloat16)
    if earlier:
        step_all(earlier["up"], upstream[:8, :128])
        step_all(earlier["down"], upstream[:8, :128])
    gate_grad = jnp.sum(upstream * combined, axis=-1, keepdims=True)
    logit_grad = gate_grad * gate_prob * (picked_expert - router_probs)
    router_term = jnp.dot(second.astype(jnp.float32).T, logit_grad, precision=PRECISE)
    second_grad = jnp.dot(logit_grad, router_weight.astype(jnp.float32).T, precision=PRECISE)
    slot_grad = jnp.dot(slot_indicator, combined_grad).reshape(EXPERTS, CAP_PADDED, model_width)
    active_grad = jnp.einsum(
        "ecd,efd->ecf", slot_grad, expert_down, preferred_element_type=jnp.float32
    )
    hidden_grad = jax.vjp(gelu_tanh, hidden)[1](active_grad)[0].astype(jnp.bfloat16)
    dispatch_grad = jnp.einsum(
        "ecf,edf->ecd", hidden_grad, expert_up, preferred_element_type=jnp.float32
    )
    second_grad = second_grad + exchange_sum(
        rows_of_slots(slot_indicator, dispatch_grad.reshape(-1, model_width))
    )
    slot_grad_ordered = jnp.dot(slot_grad, order)
    dispatched_ordered = jnp.dot(dispatched, order)

    def expert_term(ordered, hidden_rows):
        def term_of(low, high):
            return jnp.einsum(
                "cd,cf->df", ordered[:, low:high], hidden_rows, preferred_element_type=jnp.float32
            )

        return ScatterSum(term_of, model_width)

    groups = {
        "down": [expert_term(slot_grad_ordered[at], active[at]) for at in range(EXPERTS)],
        "up": [expert_term(dispatched_ordered[at], hidden_grad[at]) for at in range(EXPERTS)],
    }
    step_all(groups["down"])
    step_all(groups["up"])
    expert_done = second_grad[:8, :128]
    step_all(groups["down"], expert_done)
    if earlier:
        step_all(earlier["heads"], expert_done)
        step_all(earlier["up"], expert_done)
        step_all(earlier["down"], expert_done)
    middle_grad, midnorm_term = jax.vjp(rms_norm, middle, midnorm_gain.astype(jnp.float32))[1](
        second_grad
    )
    middle_grad = upstream + middle_grad
    attn_grad = middle_grad.astype(jnp.bfloat16)
    output_sum = expert_term(jnp.dot(attn_grad, order), mixed_heads)
    output_sum.step()
    mixed_grad = jnp.einsum(
        "td,fd->tf", attn_grad, output_weight, preferred_element_type=jnp.float32
    ).astype(jnp.bfloat16)
    scores = attention_scores(query_rows, key_rows, bucket_bias_table, segment, bucket_indicator)
    attn_probs = jnp.exp(scores - log_total)
    probs_low = attn_probs.astype(jnp.bfloat16)
    query_split = query_rows.reshape(row_count, heads_here, -1)
    key_split = key_rows.reshape(row_count, heads_here, -1)
    value_split = value_rows.reshape(row_count, heads_here, -1)
    mixed_split = mixed_grad.reshape(row_count, heads_here, -1)
    probs_grad = jnp.einsum(
        "qhd,khd->hqk", mixed_split, value_split, preferred_element_type=jnp.float32
    )
    center = jnp.sum(attn_probs * probs_grad, axis=-1, keepdims=True)
    score_gradient = (attn_probs * (probs_grad - center)).astype(jnp.bfloat16)
    value_back = jnp.einsum(
        "hqk,qhd->khd", probs_low, mixed_split, preferred_element_type=jnp.float32
    )
    key_back = jnp.einsum(
        "hqk,qhd->khd", score_gradient, query_split, preferred_element_type=jnp.float32
    )
    query_back = jnp.einsum(
        "hqk,khd->qhd", score_gradient, key_split, preferred_element_type=jnp.float32
    )
    table_term = jnp.einsum(
        "esm,psm->pe", score_gradient, bucket_indicator, preferred_element_type=jnp.float32
    )
    query_back = query_back.reshape(row_count, -1).astype(jnp.bfloat16)
    key_back = key_back.reshape(row_count, -1).astype(jnp.bfloat16)
    value_back = value_back.reshape(row_count, -1).astype(jnp.bfloat16)
    projection_sum = expert_term(
        jnp.dot(normed, order), jnp.concatenate([query_back, key_back, value_back], axis=1)
    )
    projection_sum.step()
    groups["heads"] = [output_sum, projection_sum]
    normed_part = (
        jnp.einsum("tf,df->td", query_back, query_weight, preferred_element_type=jnp.float32)
        + jnp.einsum("tf,df->td", key_back, key_weight, preferred_element_type=jnp.float32)
        + jnp.einsum("tf,df->td", value_back, value_weight, preferred_element_type=jnp.float32)
    )
    if earlier:
        heads_done = normed_part[:8, :128]
        step_all(groups["up"], heads_done)
        step_all(earlier["heads"], heads_done)
        step_all(earlier["up"], heads_done)
        step_all(groups["down"], heads_done)
    normed_grad = exchange_sum(normed_part)
    stream_grad, prenorm_term = jax.vjp(rms_norm, stream, prenorm_gain.astype(jnp.float32))[1](
        normed_grad
    )
    small_terms = (prenorm_term, midnorm_term, table_term, router_term)
    return (middle_grad + stream_grad, groups, small_terms)


def finished_terms(groups, small_terms):
    for name in ("down", "up", "heads"):
        for one in groups[name]:
            while one.bit < one.size.bit_length() - 1:
                one.step()
    prenorm_term, midnorm_term, table_term, router_term = small_terms
    output_sum, projection_sum = groups["heads"]
    query_term, key_term, value_term = jnp.split(projection_sum.kept, 3, axis=1)
    return (
        query_term,
        key_term,
        value_term,
        output_sum.kept.T,
        prenorm_term,
        midnorm_term,
        table_term,
        router_term,
        jnp.stack([one.kept for one in groups["up"]]),
        jnp.stack([one.kept.T for one in groups["down"]]),
    )


def on_device(
    tokens,
    query_weight,
    key_weight,
    value_weight,
    output_weight,
    prenorm_gain,
    midnorm_gain,
    bucket_bias_table,
    router_weight,
    expert_up,
    expert_down,
    lengths,
    expert_ids,
    cotangent,
):
    row_count = tokens.shape[0]
    segment, alive_rows = segments(lengths[0], row_count)
    expert_pick = expert_ids[:, 0]
    expert_slot_index = slot_of(expert_pick, alive_rows)
    flat_slot = jnp.where(
        expert_slot_index < CAP, expert_pick * CAP_PADDED + expert_slot_index, -1
    )
    slot_indicator = (
        jnp.arange(EXPERTS * CAP_PADDED, dtype=jnp.int32)[:, None] == flat_slot[None, :]
    ).astype(jnp.bfloat16)
    order = relative_order(tokens.shape[1])
    position = jnp.arange(row_count, dtype=jnp.int32)
    bucket_map = bucket_ids(position, position)
    bucket_indicator = (
        bucket_map[None] == jnp.arange(POSITION_BUCKETS, dtype=jnp.int32)[:, None, None]
    ).astype(jnp.bfloat16)
    weight_all = (
        query_weight,
        key_weight,
        value_weight,
        output_weight,
        prenorm_gain,
        midnorm_gain,
        bucket_bias_table,
        router_weight,
        expert_up,
        expert_down,
    )
    stream = tokens.astype(jnp.float32)
    saved_list = []
    for layer_index in range(LAYERS):
        weight_set = tuple((weight_arr[layer_index] for weight_arr in weight_all))
        saved_state, stream = forward_layer(
            stream, weight_set, segment, expert_pick, slot_indicator, bucket_indicator
        )
        saved_list.append(saved_state)
    upstream = cotangent.astype(jnp.float32) * alive_rows[:, None].astype(jnp.float32)
    layer_sums = [None] * LAYERS
    groups = None
    for layer_index in reversed(range(LAYERS)):
        weight_set = tuple((weight_arr[layer_index] for weight_arr in weight_all))
        upstream, groups, small_terms = layer_backward_pass(
            upstream,
            saved_list[layer_index],
            weight_set,
            segment,
            expert_pick,
            slot_indicator,
            bucket_indicator,
            order,
            groups,
        )
        layer_sums[layer_index] = (groups, small_terms)
    layer_terms = [None] * LAYERS
    for layer_index in reversed(range(LAYERS)):
        layer_terms[layer_index] = finished_terms(*layer_sums[layer_index])
    (
        query_weight_grad,
        key_grad,
        value_grad,
        output_grad,
        prenorm_grad,
        midnorm_grad,
        table_grad,
        router_grad,
        expert_up_grad,
        down_grad,
    ) = tuple(
        (
            jnp.stack([layer_terms[layer_index][member] for layer_index in range(LAYERS)])
            for member in range(10)
        )
    )
    model_width = tokens.shape[1]
    heads_here = bucket_bias_table.shape[2]
    small = jnp.concatenate(
        [
            prenorm_grad,
            midnorm_grad,
            router_grad.transpose(2, 0, 1).reshape(EXPERTS * LAYERS, model_width),
            jnp.pad(
                table_grad.reshape(LAYERS, -1),
                ((0, 0), (0, model_width - POSITION_BUCKETS * heads_here)),
            ),
        ]
    )
    small = doubling_sum(small)
    width = model_width // lax.axis_size("dp")
    own = lax.dynamic_slice_in_dim(
        small[: (2 + EXPERTS) * LAYERS], lax.axis_index("dp") * width, width, axis=1
    )
    prenorm_grad = own[:LAYERS]
    midnorm_grad = own[LAYERS : 2 * LAYERS]
    router_grad = own[2 * LAYERS :].reshape(EXPERTS, LAYERS, width).transpose(1, 2, 0)
    table_grad = small[(2 + EXPERTS) * LAYERS :, : POSITION_BUCKETS * heads_here].reshape(
        LAYERS, POSITION_BUCKETS, heads_here
    )
    return (
        stream.astype(jnp.bfloat16),
        upstream,
        query_weight_grad,
        key_grad,
        value_grad,
        output_grad,
        prenorm_grad,
        midnorm_grad,
        table_grad,
        router_grad,
        expert_up_grad,
        down_grad,
    )


def solution(mesh):
    return jax.shard_map(
        on_device,
        mesh=mesh,
        in_specs=(
            P("dp", None),
            P(None, None, "tensor"),
            P(None, None, "tensor"),
            P(None, None, "tensor"),
            P(None, "tensor", None),
            P(),
            P(),
            P(None, None, "tensor"),
            P(),
            P(None, None, None, "tensor"),
            P(None, None, "tensor", None),
            P("dp", None),
            P("dp", None),
            P("dp", None),
        ),
        out_specs=(
            P("dp", None),
            P("dp", None),
            P(None, "dp", "tensor"),
            P(None, "dp", "tensor"),
            P(None, "dp", "tensor"),
            P(None, "tensor", "dp"),
            P(None, "dp"),
            P(None, "dp"),
            P(None, None, "tensor"),
            P(None, "dp", None),
            P(None, None, "dp", "tensor"),
            P(None, None, "tensor", "dp"),
        ),
        check_vma=False,
    )
```
